32 devices in a mesh: dp: 2 (over y), ctx: 4 (over x, core), head: 4 (over z).
Axes of the slice: x: 2, y: 2, z: 4, core: 2. Of those that a mesh axis runs over, the one named last changes fastest.
Arguments:
- mix_query: bfloat16 [4096, 8192], P(('dp', 'ctx', 'head')), parts along dimension 0, may hold values from -6 to 6
- mix_key: bfloat16 [4096, 8192], P(('dp', 'ctx', 'head')), parts along dimension 0, may hold values from -6 to 6
- mix_value: bfloat16 [4096, 8192], P(('dp', 'ctx', 'head')), parts along dimension 0, may hold values from -6 to 6
- mr_filter: bfloat16 [512, 128], replicated, may hold values from -0.5 to 0.5
- doc_ids: int32 [4096], P('dp'), parts along dimension 0, may hold values from 0 to 3, never falling along the last dimension, each value on 1 to 1536 neighbouring positions
- att_query: bfloat16 [4096, 4096], P(('dp', 'ctx'), 'head'), parts along dimension 0, may hold values from -5 to 5
- att_key: bfloat16 [4096, 4096], P(('dp', 'ctx'), 'head'), parts along dimension 0, may hold values from -5 to 5
- att_value: bfloat16 [4096, 4096], P(('dp', 'ctx'), 'head'), parts along dimension 0, may hold values from -6 to 6
Outputs:
- mixed: bfloat16 [4096, 8192], P(('dp', 'ctx', 'head')), parts along dimension 0
- attended: bfloat16 [4096, 4096], P(('dp', 'ctx'), 'head'), parts along dimension 0
The draws below stay inside these ranges and needn't reach their ends.
There are 2 independent parts, one for each index of `dp`. The reference program is written for one: setup_inputs(seed, part) draws one part's arguments, and reference() takes and returns one part's arrays. A program takes and returns all parts, laid end to end along the dimension named above; an argument that names none is the same for every part. Nothing has to cross between parts.
Inputs may be any that keep to these rules, and one draw needn't show every extreme that they name: `doc_ids`: document numbers never fall along the sequence; every number occurs; each document covers 1 to 1536 tokens and one covers exactly 1536.
All inputs are finite; a program needn't handle non-finite values.
Results may differ from the reference program's by a relative error of at most 0.0049.
Values may be sent and summed in bfloat16 or wider, within the bound.
A program may use at most 128 MiB of HBM per device.

```python
import math
import jax
import jax.numpy as jnp
import numpy as np
from jax import lax

D = 8192
GROUPS = 512
FILT = 128
HEADS = 32
HEAD_DIM = 128
DOCS = 4
SEQ = 2048
LONGEST = 1536


def base_draw(key, salt_value):
    row_width = HEADS * HEAD_DIM
    return jnp.clip(jax.random.normal(jax.random.fold_in(key, salt_value), (SEQ, row_width), jnp.float32), -5.0, 5.0)


def draw_att_query(key, part):
    values_out = base_draw(key, 1)
    return values_out.astype(jnp.bfloat16)


def draw_att_key(key, part):
    values_out = base_draw(key, 2)
    return values_out.astype(jnp.bfloat16)


def level_of(stream_key, shape, split, least, top_value):
    def one(position, blocks):
        heights = jax.random.uniform(jax.random.fold_in(jax.random.fold_in(stream_key, 6), position), (blocks,), jnp.float32, least / len(split), top_value / len(split))
        return jnp.repeat(jnp.exp(heights), shape[position] // blocks).reshape((-1,) + (1,) * (len(shape) - position - 1))

    level = one(*split[0])
    for cut in split[1:]:
        level = level * one(*cut)
    return level


def profile(number_of, total, limit, skew):
    weights = [(1 << 20) // math.isqrt(grade ** skew) + 1 for grade in range(2, number_of + 1)]
    rest, holding = total - limit - (number_of - 1), [1] * (number_of - 1)
    while rest > 0:
        free = [i for i in range(number_of - 1) if holding[i] < limit]
        pool, budget = sum([weights[i] for i in free]), rest
        for i in free:
            extra = min(limit - holding[i], max(1, budget * weights[i] // pool), rest)
            holding[i] = holding[i] + extra
            rest = rest - extra
    return np.array([limit] + holding)


def uneven(rng, number_of, total, most, slope):
    if number_of == 2:
        one = jax.random.randint(rng, (), max(1, total - most), min(most, total - 1) + 1)
        return jnp.stack([one, total - one])
    tallies = jnp.asarray(profile(number_of, total, most, slope), jnp.int32)
    couples = (number_of - 1) // 2
    source_of, receiver = tallies[1:1 + 2 * couples:2], tallies[2:2 + 2 * couples:2]
    margin = jnp.minimum(source_of - 1, most - receiver)
    shifted = jax.random.randint(jax.random.fold_in(rng, 1), (couples,), 0, 1 << 20) % (margin + 1)
    tallies = tallies.at[1:1 + 2 * couples:2].set(source_of - shifted).at[2:2 + 2 * couples:2].set(receiver + shifted)
    return tallies[jax.random.permutation(jax.random.fold_in(rng, 2), number_of)]


def normal_values(key, shape, spread, limit, shards=(), kind=jnp.bfloat16):
    result = spread * jax.random.normal(key, shape, jnp.float32)
    if shards:
        result = result * level_of(key, shape, shards, -0.22, 0.18)
    return jnp.clip(result, -limit, limit).astype(kind)


def setup_inputs(seed: int = 0, part: int = 0) -> dict:
    seeds = jax.random.split(jax.random.key(seed), 9)
    part_splits = jax.random.split(jax.random.fold_in(seeds[8], part), 9)
    mix_query = normal_values(part_splits[0], (SEQ, D), 1.0, 6.0, ((0, 16),))
    mix_key = normal_values(part_splits[1], (SEQ, D), 1.0, 6.0, ((0, 16),))
    mix_value = normal_values(part_splits[2], (SEQ, D), 1.0, 6.0, ((0, 16),))
    mr_filter = normal_values(seeds[3], (GROUPS, FILT), FILT ** -0.5, 0.5)
    doc_ids = jnp.searchsorted(jnp.cumsum(uneven(part_splits[4], DOCS, SEQ, LONGEST, 0)), jnp.arange(SEQ), side="right").astype(jnp.int32)
    att_query = draw_att_query(jax.random.fold_in(jax.random.fold_in(seeds[8], part), 71), part)
    att_key = draw_att_key(jax.random.fold_in(jax.random.fold_in(seeds[8], part), 71), part)
    att_value = normal_values(part_splits[7], (SEQ, HEADS * HEAD_DIM), 1.0, 6.0, ((0, 4), (1, 4)))
    return {"mix_query": mix_query, "mix_key": mix_key, "mix_value": mix_value, "mr_filter": mr_filter, "doc_ids": doc_ids, "att_query": att_query, "att_key": att_key, "att_value": att_value}


NEG_FILL = -1e+30

def toeplitz_rows(filters):
    groups = filters.shape[0]
    filt_len = filters.shape[1]
    lag_index = jnp.arange(filt_len, dtype=jnp.int32)[:, None, None]
    out_index = jnp.arange(filt_len, dtype=jnp.int32)[None, :, None]
    src_index = jnp.arange(2 * filt_len, dtype=jnp.int32)[None, None, :]
    table = (out_index + filt_len - src_index == lag_index).astype(filters.dtype)
    table = table.reshape(filt_len, 2 * filt_len * filt_len)
    kernel = jnp.dot(filters, table, preferred_element_type=jnp.float32).astype(filters.dtype)
    return kernel.reshape(groups, filt_len, 2 * filt_len)

def grouped_conv(extended, seg_ext, filters):
    groups = filters.shape[0]
    filt_len = filters.shape[1]
    channels = extended.shape[1]
    group_size = channels // groups
    blocks = extended.shape[0] // filt_len - 1
    tiled_rows = extended.reshape(blocks + 1, filt_len, groups, group_size)
    paired = jnp.concatenate([tiled_rows[:-1], tiled_rows[1:]], axis=1)
    seg_tiles = seg_ext.reshape(blocks + 1, filt_len)
    seg_pairs = jnp.concatenate([seg_tiles[:-1], seg_tiles[1:]], axis=1)
    same_doc = seg_tiles[1:][:, :, None] == seg_pairs[:, None, :]
    group_step = math.gcd(groups, 64)
    group_blocks = groups // group_step
    pairs_split = jnp.moveaxis(paired.reshape(blocks, 2 * filt_len, group_blocks, group_step, group_size), 2, 0)
    filt_split = filters.reshape(group_blocks, group_step, filt_len)

    def per_groups(operands):
        part_filters, part_pairs = operands
        kernel = toeplitz_rows(part_filters).astype(jnp.float32)
        masked = jnp.where(same_doc[:, None], kernel[None], jnp.zeros((), jnp.float32))
        return jnp.einsum('bgts,bsgc->btgc', masked, part_pairs.astype(jnp.float32), precision=lax.Precision.HIGHEST)
    results = lax.map(per_groups, (filt_split, pairs_split))
    return jnp.moveaxis(results, 0, 2).reshape(blocks * filt_len, channels)

def reference(mix_query, mix_key, mix_value, mr_filter, doc_ids, att_query, att_key, att_value):
    product = (mix_key.astype(jnp.float32) * mix_value.astype(jnp.float32)).astype(jnp.bfloat16)
    filt_len = mr_filter.shape[1]
    extended = jnp.concatenate([jnp.zeros((filt_len, D), jnp.bfloat16), product], axis=0)
    seg_ext = jnp.concatenate([jnp.full((filt_len,), -1, jnp.int32), doc_ids.astype(jnp.int32)])
    convolved = grouped_conv(extended, seg_ext, mr_filter)
    mixed = (mix_query.astype(jnp.float32) * convolved).astype(jnp.bfloat16)
    head_count = att_query.shape[1] // HEAD_DIM
    score_scale = 1.0 / math.sqrt(HEAD_DIM)

    def split_heads(array):
        return jnp.moveaxis(array.reshape(SEQ, head_count, HEAD_DIM), 1, 0)
    positions = jnp.arange(SEQ, dtype=jnp.int32)
    allowed = (positions[None, :] <= positions[:, None]) & (doc_ids[None, :] == doc_ids[:, None])

    def per_head(operands):
        query_head, key_head, value_head = operands
        scores = jnp.dot(query_head, key_head.T, preferred_element_type=jnp.float32) * score_scale
        masked = jnp.where(allowed, scores, NEG_FILL)
        row_max = lax.optimization_barrier(jnp.max(masked, axis=1, keepdims=True))
        weights = jnp.where(allowed, jnp.exp(masked - row_max), 0.0)
        denominator = lax.optimization_barrier(jnp.sum(weights, axis=1, keepdims=True))
        summed = jnp.dot(weights.astype(jnp.bfloat16), value_head, preferred_element_type=jnp.float32)
        return (summed / denominator).astype(jnp.bfloat16)
    outputs = lax.map(per_head, (split_heads(att_query), split_heads(att_key), split_heads(att_value)))
    attended = jnp.moveaxis(outputs, 0, 1).reshape(SEQ, head_count * HEAD_DIM)
    return (mixed, attended)
```

```python
import functools
import math

import jax
import jax.numpy as jnp
from jax import lax
from jax.experimental import pallas as pl
from jax.experimental.pallas import tpu as pltpu
from jax.sharding import PartitionSpec as P

HEAD_DIM = 128
NEG_FILL = -1e30
SCALE2 = math.log2(math.e) / math.sqrt(HEAD_DIM)
MIX_CHUNKS = 4
HEAD_CHUNKS = 2
VMEM_BYTES = 48 * 1024 * 1024


def conv_kernel(groups, filt_ref, mask_ref, prev_ref, cur_ref, gate_ref, *rest):
    out_ref = rest[-1]
    taps = filt_ref.shape[1]
    lanes = prev_ref.shape[1]
    size = lanes // groups
    mask = mask_ref[...]
    filters = filt_ref[...].astype(jnp.float32)
    prev_t = prev_ref[...].astype(jnp.float32).T
    cur_t = cur_ref[...].astype(jnp.float32).T
    rows = jnp.concatenate([prev_t, cur_t], axis=1).astype(jnp.bfloat16)
    pieces = []
    for g in range(groups):
        row = jnp.broadcast_to(filters[g : g + 1], (taps, taps))
        ring = pltpu.roll(row, 0, 1, stride=1, stride_axis=0).astype(jnp.bfloat16)
        weight = jnp.concatenate([ring, ring], axis=0) * mask
        pieces.append(
            jnp.dot(
                rows[g * size : (g + 1) * size], weight, preferred_element_type=jnp.float32
            )
        )
    convolved = jnp.concatenate(pieces, axis=0).T
    out_ref[...] = (gate_ref[...].astype(jnp.float32) * convolved).astype(out_ref.dtype)


def convolve(chunk, filters, mask, prev, cur, gate, so_far):
    rows, width = prev.shape
    total = gate.shape[1]
    group_size = total // filters.shape[0]
    lanes = 128
    groups = lanes // group_size
    steps = width // lanes
    first = chunk * steps
    in_specs = [
        pl.BlockSpec((groups, filters.shape[1]), lambda i: (first + i, 0)),
        pl.BlockSpec(mask.shape, lambda i: (0, 0)),
        pl.BlockSpec((rows, lanes), lambda i: (0, i)),
        pl.BlockSpec((rows, lanes), lambda i: (0, i)),
        pl.BlockSpec((rows, lanes), lambda i: (0, first + i)),
    ]
    operands = [filters, mask, prev, cur, gate]
    aliases = {}
    if so_far is not None:
        in_specs.append(pl.BlockSpec(memory_space=pl.ANY))
        operands.append(so_far)
        aliases = {5: 0}
    return pl.pallas_call(
        functools.partial(conv_kernel, groups),
        grid=(steps,),
        out_shape=jax.ShapeDtypeStruct(gate.shape, gate.dtype),
        in_specs=in_specs,
        out_specs=pl.BlockSpec((rows, lanes), lambda i: (0, first + i)),
        input_output_aliases=aliases,
        compiler_params=pltpu.CompilerParams(vmem_limit_bytes=VMEM_BYTES),
        cost_estimate=pl.CostEstimate(
            flops=2 * rows * 2 * rows * 256 * width // group_size,
            bytes_accessed=4 * rows * width * 2,
            transcendentals=0,
        ),
    )(*operands)


def softmax_part(query, key, value, bias):
    scores = lax.dot_general(
        query, key, (((1,), (1,)), ((), ())), preferred_element_type=jnp.float32
    )
    scores = scores + bias
    top = jnp.max(scores, axis=1, keepdims=True)
    weights = jnp.exp2((scores - top) * SCALE2)
    total = jnp.sum(weights, axis=1, keepdims=True)
    summed = jnp.dot(weights.astype(jnp.bfloat16), value, preferred_element_type=jnp.float32)
    return summed / total, top * SCALE2 + jnp.log2(total)


def as_row(column):
    wide = jnp.broadcast_to(column, (column.shape[0], HEAD_DIM))
    return wide.T[0:1]


def attend_kernel(
    how_ref, low_ref, high_ref, kpos_ref, q_ref, k_own, v_own, k_far, v_far, o_ref, lse_ref, bias
):
    how = how_ref[0]
    head = pl.program_id(0)
    own = k_own.shape[0]

    @pl.when((head == 0) & (how > 0))
    def _():
        kpos = kpos_ref[...]
        allowed = (kpos >= low_ref[...]) & (kpos <= high_ref[...])
        bias[...] = jnp.where(allowed, 0.0, NEG_FILL)

    @pl.when(how == 1)
    def _():
        out, lse = softmax_part(q_ref[...], k_own[...], v_own[...], bias[:, :own])
        o_ref[...] = out.astype(o_ref.dtype)
        lse_ref[pl.ds(head, 1), :] = as_row(lse)

    @pl.when(how == 2)
    def _():
        key = jnp.concatenate([k_own[...], k_far[...]], axis=0)
        value = jnp.concatenate([v_own[...], v_far[...]], axis=0)
        out, lse = softmax_part(q_ref[...], key, value, bias[...])
        o_ref[...] = out.astype(o_ref.dtype)
        lse_ref[pl.ds(head, 1), :] = as_row(lse)


def attend(how, low, high, kpos, query, own, far, first, out_type):
    rows, width = query.shape
    heads = width // HEAD_DIM
    keys = own[0].shape[0]
    here = pl.BlockSpec((rows, HEAD_DIM), lambda h: (0, h))
    there = pl.BlockSpec((keys, HEAD_DIM), lambda h: (0, first + h))
    whole = lambda shape: pl.BlockSpec(shape, lambda h: (0, 0))
    return pl.pallas_call(
        attend_kernel,
        grid=(heads,),
        out_shape=(
            jax.ShapeDtypeStruct((rows, width), out_type),
            jax.ShapeDtypeStruct((heads, rows), jnp.float32),
        ),
        in_specs=[
            pl.BlockSpec(memory_space=pltpu.SMEM),
            whole(low.shape),
            whole(high.shape),
            whole(kpos.shape),
            here,
            there,
            there,
            there,
            there,
        ],
        out_specs=(here, whole((heads, rows))),
        scratch_shapes=[pltpu.VMEM((rows, 2 * keys), jnp.float32)],
        compiler_params=pltpu.CompilerParams(vmem_limit_bytes=VMEM_BYTES),
        cost_estimate=pl.CostEstimate(
            flops=4 * rows * 2 * keys * width,
            bytes_accessed=8 * rows * width,
            transcendentals=heads * rows * 2 * keys,
        ),
    )(how, low, high, kpos, query, *own, *far)


def merge_kernel(heads, has_ref, o1_ref, l1_ref, o2_ref, l2_ref, out_ref):
    has = has_ref[0]

    @pl.when(has == 0)
    def _():
        out_ref[...] = o1_ref[...].astype(out_ref.dtype)

    @pl.when(has != 0)
    def _():
        first, second = l1_ref[...], l2_ref[...]
        top = jnp.maximum(first, second)
        one, two = jnp.exp2(first - top), jnp.exp2(second - top)
        share = two / (one + two)
        for h in range(heads):
            cols = slice(h * HEAD_DIM, (h + 1) * HEAD_DIM)
            part = jnp.broadcast_to(share[h : h + 1], (HEAD_DIM, share.shape[1])).T
            base = o1_ref[:, cols]
            out_ref[:, cols] = (
                base + (o2_ref[:, cols].astype(jnp.float32) - base) * part
            ).astype(out_ref.dtype)


def merge(has, local, far):
    rows, width = local[0].shape
    heads = width // HEAD_DIM
    vmem = pl.BlockSpec(memory_space=pltpu.VMEM)
    return pl.pallas_call(
        functools.partial(merge_kernel, heads),
        out_shape=jax.ShapeDtypeStruct((rows, width), jnp.bfloat16),
        in_specs=[pl.BlockSpec(memory_space=pltpu.SMEM)] + [vmem] * 4,
        out_specs=vmem,
        compiler_params=pltpu.CompilerParams(vmem_limit_bytes=VMEM_BYTES),
        cost_estimate=pl.CostEstimate(
            flops=4 * rows * width, bytes_accessed=8 * rows * width, transcendentals=0
        ),
    )(has, *local, *far)


def on_device(mix_query, mix_key, mix_value, mr_filter, doc_ids, att_query, att_key, att_value):
    ctx = lax.axis_index("ctx")
    ctx_size = lax.axis_size("ctx")
    half = ctx_size // 2
    assert ctx_size == 4
    swap = [(i, i ^ 1) for i in range(ctx_size)]
    back = [(i + half, i) for i in range(half)]
    forth = [(i, i + half) for i in range(half)]

    rows, width = att_query.shape
    part = width // HEAD_CHUNKS
    far_queries = [
        lax.ppermute(att_query[:, c * part : (c + 1) * part], "ctx", back)
        for c in range(HEAD_CHUNKS)
    ]
    far = (lax.ppermute(att_key, "ctx", swap), lax.ppermute(att_value, "ctx", swap))
    own = (att_key, att_value)

    tok_rows, channels = mix_query.shape
    chunk = channels // MIX_CHUNKS
    peers = ctx_size * lax.axis_size("head")
    onward = [(i, i + 1) for i in range(peers - 1)]
    products, rims = [], []
    for c in range(MIX_CHUNKS):
        cols = slice(c * chunk, (c + 1) * chunk)
        product = (
            mix_key[:, cols].astype(jnp.float32) * mix_value[:, cols].astype(jnp.float32)
        ).astype(jnp.bfloat16)
        products.append(product)
        rims.append(lax.ppermute(product, ("ctx", "head"), onward))

    seq = doc_ids.shape[0]
    positions = jnp.arange(seq, dtype=jnp.int32)
    starts = jnp.sum(
        (doc_ids[None, :] < doc_ids[:, None]).astype(jnp.int32), axis=1, dtype=jnp.int32
    )

    def of_block(block):
        begin = block * rows
        low = lax.dynamic_slice_in_dim(starts, begin, rows)
        return low[:, None], (begin + jnp.arange(rows, dtype=jnp.int32))[:, None]

    offset = jnp.arange(rows, dtype=jnp.int32)
    kpos = jnp.concatenate([ctx * rows + offset, (ctx ^ 1) * rows + offset])[None]
    local_how = jnp.where(ctx % 2 == 1, 2, 1).astype(jnp.int32)[None]
    far_how = jnp.where(ctx < half, 2, 0).astype(jnp.int32)[None]
    has = (ctx >= half).astype(jnp.int32)[None]
    local_rows = of_block(ctx)
    far_rows = of_block(jnp.minimum(ctx + half, ctx_size - 1))
    heads = part // HEAD_DIM
    partials = []
    for c in range(HEAD_CHUNKS):
        out, lse = attend(
            far_how, *far_rows, kpos, far_queries[c], own, far, c * heads, jnp.bfloat16
        )
        partials.append((lax.ppermute(out, "ctx", forth), lax.ppermute(lse, "ctx", forth)))
    merged = []
    for c in range(HEAD_CHUNKS):
        query = att_query[:, c * part : (c + 1) * part]
        local = attend(local_how, *local_rows, kpos, query, own, far, c * heads, jnp.float32)
        merged.append(merge(has, local, partials[c]))
    attended = jnp.concatenate(merged, axis=1)

    taps = mr_filter.shape[1]
    place = (ctx * lax.axis_size("head") + lax.axis_index("head")) * tok_rows
    padded_ids = jnp.concatenate([jnp.full((taps,), -1, jnp.int32), doc_ids])
    near_ids = lax.dynamic_slice_in_dim(padded_ids, place, tok_rows + taps)
    lag = jnp.arange(tok_rows)[None, :] + taps - jnp.arange(tok_rows + taps)[:, None]
    mask = (
        (lag >= 0) & (lag < taps) & (near_ids[:, None] == near_ids[None, taps:])
    ).astype(jnp.bfloat16)
    mixed = None
    for c in range(MIX_CHUNKS):
        mixed = convolve(c, mr_filter, mask, rims[c], products[c], mix_query, mixed)
    return (mixed, attended)


def solution(mesh):
    placed = (
        P(("dp", "ctx", "head"), None),
        P(("dp", "ctx", "head"), None),
        P(("dp", "ctx", "head"), None),
        P(),
        P("dp"),
        P(("dp", "ctx"), "head"),
        P(("dp", "ctx"), "head"),
        P(("dp", "ctx"), "head"),
    )
    return jax.shard_map(
        on_device,
        mesh=mesh,
        in_specs=placed,
        out_specs=(P(("dp", "ctx", "head"), None), P(("dp", "ctx"), "head")),
        check_vma=False,
    )
```

```python
import functools
import math

import jax
import jax.numpy as jnp
from jax import lax
from jax.experimental import pallas as pl
from jax.experimental.pallas import tpu as pltpu
from jax.sharding import PartitionSpec as P

HEAD_DIM = 128
DOCS = 4
NEG_FILL = -1e30
SCALE2 = math.log2(math.e) / math.sqrt(HEAD_DIM)
MIX_CHUNKS = 2
HEAD_CHUNKS = 2
STEP = 32
VMEM_BYTES = 48 * 1024 * 1024


def conv_kernel(groups, filt_ref, mask_ref, prev_ref, cur_ref, gate_ref, *rest):
    out_ref = rest[-1]
    taps = filt_ref.shape[1]
    lanes = prev_ref.shape[1]
    size = lanes // groups
    few = 16
    mask = mask_ref[...]
    filters = filt_ref[...].astype(jnp.float32)
    rows = jnp.concatenate([prev_ref[...].T, cur_ref[...].T], axis=1)

    def weight(g):
        row = jnp.broadcast_to(filters[g : g + 1], (few, taps))
        base = pltpu.roll(row, 0, 1, stride=1, stride_axis=0).astype(jnp.bfloat16)
        turns = [base] + [pltpu.roll(base, i, 1) for i in range(few, taps, few)]
        return jnp.concatenate(turns + turns, axis=0) * mask

    pieces = []
    for g in range(0, groups, 2):
        pair = jnp.concatenate([weight(g), weight(g + 1)], axis=1)
        both = jnp.dot(
            rows[g * size : (g + 2) * size], pair, preferred_element_type=jnp.float32
        )
        pieces += [both[:size, :taps], both[size:, taps:]]
    convolved = jnp.concatenate(pieces, axis=0).T
    out_ref[...] = (gate_ref[...].astype(jnp.float32) * convolved).astype(out_ref.dtype)


def convolve(chunk, filters, mask, prev, cur, gate, so_far):
    rows, width = prev.shape
    total = gate.shape[1]
    group_size = total // filters.shape[0]
    lanes = 512
    groups = lanes // group_size
    steps = width // lanes
    first = chunk * steps
    in_specs = [
        pl.BlockSpec((groups, filters.shape[1]), lambda i: (first + i, 0)),
        pl.BlockSpec(mask.shape, lambda i: (0, 0)),
        pl.BlockSpec((rows, lanes), lambda i: (0, i)),
        pl.BlockSpec((rows, lanes), lambda i: (0, i)),
        pl.BlockSpec((rows, lanes), lambda i: (0, first + i)),
    ]
    operands = [filters, mask, prev, cur, gate]
    aliases = {}
    if so_far is not None:
        in_specs.append(pl.BlockSpec(memory_space=pl.ANY))
        operands.append(so_far)
        aliases = {5: 0}
    return pl.pallas_call(
        functools.partial(conv_kernel, groups),
        grid=(steps,),
        out_shape=jax.ShapeDtypeStruct(gate.shape, gate.dtype),
        in_specs=in_specs,
        out_specs=pl.BlockSpec((rows, lanes), lambda i: (0, first + i)),
        input_output_aliases=aliases,
        compiler_params=pltpu.CompilerParams(vmem_limit_bytes=VMEM_BYTES),
        cost_estimate=pl.CostEstimate(
            flops=2 * rows * 2 * rows * 256 * width // group_size,
            bytes_accessed=4 * rows * width * 2,
            transcendentals=0,
        ),
    )(*operands)


def three_terms(x):
    high = x.astype(jnp.bfloat16).astype(jnp.float32)
    middle = (x - high).astype(jnp.bfloat16).astype(jnp.float32)
    return high, middle, x - high - middle


def attend_tiles(head, causal, use_far, q_ref, k_own, v_own, k_far, v_far, *refs):
    bias = refs[-1]
    out_ref = refs[-2]
    terms = out_ref.dtype == jnp.bfloat16
    stats = slice(out_ref.shape[1] - HEAD_DIM, out_ref.shape[1])
    place = pl.ds(pl.multiple_of(head * HEAD_DIM, HEAD_DIM), HEAD_DIM)
    own = k_own.shape[0]
    tile = 128
    count = q_ref.shape[0] // tile
    ones = jnp.ones((own, HEAD_DIM), jnp.bfloat16)
    wide_own = jnp.concatenate([v_own[...], ones], axis=1)
    wide_far = jnp.concatenate([v_far[...], ones], axis=1)
    lane = lax.broadcasted_iota(jnp.int32, (tile, HEAD_DIM), 1)

    def scores_of(i):
        here = slice(i * tile, (i + 1) * tile)
        seen = (i + 1) * tile if causal else own
        query = q_ref[here]
        dims = (((1,), (1,)), ((), ()))
        near = lax.dot_general(
            query, k_own[:seen], dims, preferred_element_type=jnp.float32
        )
        out = [near + bias[here, :seen]]
        if use_far:
            away = lax.dot_general(query, k_far[...], dims, preferred_element_type=jnp.float32)
            out.append(away + bias[here, own:])
        return out

    def finish(i, scores):
        here = slice(i * tile, (i + 1) * tile)
        top = jnp.max(scores[0], axis=1, keepdims=True)
        if use_far:
            top = jnp.maximum(top, jnp.max(scores[1], axis=1, keepdims=True))
        weights = [jnp.exp2((s - top) * SCALE2).astype(jnp.bfloat16) for s in scores]
        both = jnp.dot(
            weights[0], wide_own[: scores[0].shape[1]], preferred_element_type=jnp.float32
        )
        if use_far:
            both += jnp.dot(weights[1], wide_far, preferred_element_type=jnp.float32)
        total = both[:, HEAD_DIM:]
        out_ref[here, place] = (both[:, :HEAD_DIM] / total).astype(out_ref.dtype)
        lse = top * SCALE2 + jnp.log2(total)
        spread = out_ref[here, stats].astype(jnp.float32)
        if terms:
            for at, term in enumerate(three_terms(lse)):
                spread = jnp.where(lane == head + at * STEP, term, spread)
        else:
            spread = jnp.where(lane == head, lse, spread)
        out_ref[here, stats] = spread.astype(out_ref.dtype)

    ready = scores_of(0)
    for i in range(count):
        later = scores_of(i + 1) if i + 1 < count else None
        finish(i, ready)
        ready = later


def attend_kernel(causal, how_ref, low_ref, high_ref, kpos_ref, *refs):
    how = how_ref[0]
    head = pl.program_id(0)
    bias = refs[-1]

    @pl.when(head == 0)
    def _():
        out_ref = refs[-2]
        out_ref[...] = jnp.zeros_like(out_ref)

    @pl.when((head == 0) & (how > 0))
    def _():
        kpos = kpos_ref[...]
        allowed = (kpos >= low_ref[...]) & (kpos <= high_ref[...])
        bias[...] = jnp.where(allowed, 0.0, NEG_FILL)

    if causal:

        @pl.when(how == 1)
        def _():
            attend_tiles(head, causal, False, *refs)

    @pl.when(how == 2)
    def _():
        attend_tiles(head, causal, True, *refs)


def attend(how, low, high, kpos, query, own, far, first, heads, causal, out_type, after):
    rows = query.shape[0]
    width = (heads + 1) * HEAD_DIM
    keys = own[0].shape[0]
    block = pl.BlockSpec((rows, HEAD_DIM), lambda h: (0, first + h))
    whole = lambda shape: pl.BlockSpec(shape, lambda h: (0, 0))
    return pl.pallas_call(
        functools.partial(attend_kernel, causal),
        grid=(heads,),
        out_shape=jax.ShapeDtypeStruct((rows, width), out_type),
        in_specs=[
            pl.BlockSpec(memory_space=pltpu.SMEM),
            whole(low.shape),
            whole(high.shape),
            whole(kpos.shape),
        ]
        + [block] * 5
        + [pl.BlockSpec(memory_space=pl.ANY)] * len(after),
        out_specs=whole((rows, width)),
        scratch_shapes=[pltpu.VMEM((rows, 2 * keys), jnp.float32)],
        compiler_params=pltpu.CompilerParams(vmem_limit_bytes=VMEM_BYTES),
        cost_estimate=pl.CostEstimate(
            flops=12 * rows * 2 * keys * width,
            bytes_accessed=8 * rows * width,
            transcendentals=heads * rows * 2 * keys,
        ),
    )(how, low, high, kpos, query, *own, *far, *after)


def merge_kernel(heads, chunks, has_ref, o1_ref, *refs):
    out_ref = refs[-1]
    width = heads * HEAD_DIM
    has = has_ref[0]
    each = heads // chunks

    @pl.when(has == 0)
    def _():
        out_ref[...] = o1_ref[:, :width].astype(out_ref.dtype)

    @pl.when(has != 0)
    def _():
        first = o1_ref[:, width:]
        for c in range(chunks):
            o2_ref = refs[c]
            mine = first if c == 0 else pltpu.roll(first, HEAD_DIM - c * each, 1)
            sent = o2_ref[:, each * HEAD_DIM :].astype(jnp.float32)
            second = (
                sent
                + pltpu.roll(sent, HEAD_DIM - STEP, 1)
                + pltpu.roll(sent, HEAD_DIM - 2 * STEP, 1)
            )
            top = jnp.maximum(mine, second)
            one, two = jnp.exp2(mine - top), jnp.exp2(second - top)
            share = two / (one + two)
            for h in range(each):
                near = slice((c * each + h) * HEAD_DIM, (c * each + h + 1) * HEAD_DIM)
                cols = slice(h * HEAD_DIM, (h + 1) * HEAD_DIM)
                base = o1_ref[:, near]
                out_ref[:, near] = (
                    base + (o2_ref[:, cols].astype(jnp.float32) - base) * share[:, h : h + 1]
                ).astype(out_ref.dtype)


def merge(has, local, partials):
    rows = local.shape[0]
    width = local.shape[1] - HEAD_DIM
    heads = width // HEAD_DIM
    vmem = pl.BlockSpec(memory_space=pltpu.VMEM)
    return pl.pallas_call(
        functools.partial(merge_kernel, heads, len(partials)),
        out_shape=jax.ShapeDtypeStruct((rows, width), jnp.bfloat16),
        in_specs=[pl.BlockSpec(memory_space=pltpu.SMEM)] + [vmem] * (1 + len(partials)),
        out_specs=vmem,
        compiler_params=pltpu.CompilerParams(vmem_limit_bytes=VMEM_BYTES),
        cost_estimate=pl.CostEstimate(
            flops=4 * rows * width, bytes_accessed=8 * rows * width, transcendentals=0
        ),
    )(has, local, *partials)


def on_device(mix_query, mix_key, mix_value, mr_filter, doc_ids, att_query, att_key, att_value):
    ctx = lax.axis_index("ctx")
    ctx_size = lax.axis_size("ctx")
    half = ctx_size // 2
    assert ctx_size == 4
    swap = [(i, i ^ 1) for i in range(ctx_size)]
    back = [(i + half, i) for i in range(half)]
    forth = [(i, i + half) for i in range(half)]

    rows, width = att_query.shape
    far_query = lax.ppermute(att_query, "ctx", back)
    far = (lax.ppermute(att_key, "ctx", swap), lax.ppermute(att_value, "ctx", swap))
    own = (att_key, att_value)

    tok_rows, channels = mix_query.shape
    chunk = channels // MIX_CHUNKS
    peers = ctx_size * lax.axis_size("head")
    onward = [(i, i + 1) for i in range(peers - 1)]
    products, rims = [], []
    for c in range(MIX_CHUNKS):
        cols = slice(c * chunk, (c + 1) * chunk)
        product = (
            mix_key[:, cols].astype(jnp.float32) * mix_value[:, cols].astype(jnp.float32)
        ).astype(jnp.bfloat16)
        products.append(product)
        rims.append(lax.ppermute(product, ("ctx", "head"), onward))

    def of_block(block):
        begin = block * rows
        ids = lax.dynamic_slice_in_dim(doc_ids, begin, rows)
        low = jnp.zeros((rows,), jnp.int32)
        for doc in range(1, DOCS):
            before = jnp.sum((doc_ids < doc).astype(jnp.int32), dtype=jnp.int32)
            low = jnp.where(ids >= doc, before, low)
        return low[:, None], (begin + jnp.arange(rows, dtype=jnp.int32))[:, None]

    offset = jnp.arange(rows, dtype=jnp.int32)
    kpos = jnp.concatenate([ctx * rows + offset, (ctx ^ 1) * rows + offset])[None]
    local_how = jnp.where(ctx % 2 == 1, 2, 1).astype(jnp.int32)[None]
    far_how = jnp.where(ctx < half, 2, 0).astype(jnp.int32)[None]
    has = (ctx >= half).astype(jnp.int32)[None]
    local_rows = of_block(ctx)
    far_rows = of_block(jnp.minimum(ctx + half, ctx_size - 1))
    heads = width // HEAD_DIM
    each = heads // HEAD_CHUNKS
    local = attend(
        local_how, *local_rows, kpos, att_query, own, far, 0, heads, True, jnp.float32, ()
    )
    partials, after = [], (local,)
    for c in range(HEAD_CHUNKS):
        out = attend(
            far_how,
            *far_rows,
            kpos,
            far_query,
            own,
            far,
            c * each,
            each,
            False,
            jnp.bfloat16,
            after,
        )
        after = (out,)
        partials.append(lax.ppermute(out, "ctx", forth))
    attended = merge(has, local, partials)

    taps = mr_filter.shape[1]
    place = (ctx * lax.axis_size("head") + lax.axis_index("head")) * tok_rows
    padded_ids = jnp.concatenate([jnp.full((taps,), -1, jnp.int32), doc_ids])
    near_ids = lax.dynamic_slice_in_dim(padded_ids, place, tok_rows + taps)
    lag = jnp.arange(tok_rows)[None, :] + taps - jnp.arange(tok_rows + taps)[:, None]
    mask = (
        (lag >= 0) & (lag < taps) & (near_ids[:, None] == near_ids[None, taps:])
    ).astype(jnp.bfloat16)
    mixed = None
    for c in range(MIX_CHUNKS):
        mixed = convolve(c, mr_filter, mask, rims[c], products[c], mix_query, mixed)
    return (mixed, attended)


def solution(mesh):
    placed = (
        P(("dp", "ctx", "head"), None),
        P(("dp", "ctx", "head"), None),
        P(("dp", "ctx", "head"), None),
        P(),
        P("dp"),
        P(("dp", "ctx"), "head"),
        P(("dp", "ctx"), "head"),
        P(("dp", "ctx"), "head"),
    )
    return jax.shard_map(
        on_device,
        mesh=mesh,
        in_specs=placed,
        out_specs=(P(("dp", "ctx", "head"), None), P(("dp", "ctx"), "head")),
        check_vma=False,
    )
```

```python
import functools
import math

import jax
import jax.numpy as jnp
from jax import lax
from jax.experimental import pallas as pl
from jax.experimental.pallas import tpu as pltpu
from jax.sharding import PartitionSpec as P

HEAD_DIM = 128
DOCS = 4
NEG_FILL = -1e30
SCALE2 = math.log2(math.e) / math.sqrt(HEAD_DIM)
MIX_CHUNKS = 2
STEP = 32
DECLARED = 1 << 20
VMEM_BYTES = 60 * 1024 * 1024


def conv_kernel(groups, filt_ref, mask_ref, prev_ref, cur_ref, gate_ref, *rest):
    out_ref = rest[-1]
    taps = filt_ref.shape[1]
    lanes = prev_ref.shape[1]
    size = lanes // groups
    few = 16
    mask = mask_ref[...]
    filters = filt_ref[...].astype(jnp.float32)
    rows = jnp.concatenate([prev_ref[...].T, cur_ref[...].T], axis=1)

    def weight(g):
        row = jnp.broadcast_to(filters[g : g + 1], (few, taps))
        base = pltpu.roll(row, 0, 1, stride=1, stride_axis=0).astype(jnp.bfloat16)
        turns = [base] + [pltpu.roll(base, i, 1) for i in range(few, taps, few)]
        return jnp.concatenate(turns + turns, axis=0) * mask

    pieces = []
    for g in range(0, groups, 2):
        pair = jnp.concatenate([weight(g), weight(g + 1)], axis=1)
        both = jnp.dot(
            rows[g * size : (g + 2) * size], pair, preferred_element_type=jnp.float32
        )
        pieces += [both[:size, :taps], both[size:, taps:]]
    convolved = jnp.concatenate(pieces, axis=0).T
    out_ref[...] = (gate_ref[...].astype(jnp.float32) * convolved).astype(out_ref.dtype)


def convolve(chunk, filters, mask, prev, cur, gate, so_far, after):
    rows, width = prev.shape
    total = gate.shape[1]
    group_size = total // filters.shape[0]
    lanes = 512
    groups = lanes // group_size
    steps = width // lanes
    first = chunk * steps
    in_specs = [
        pl.BlockSpec((groups, filters.shape[1]), lambda i: (first + i, 0)),
        pl.BlockSpec(mask.shape, lambda i: (0, 0)),
        pl.BlockSpec((rows, lanes), lambda i: (0, i)),
        pl.BlockSpec((rows, lanes), lambda i: (0, i)),
        pl.BlockSpec((rows, lanes), lambda i: (0, first + i)),
    ]
    operands = [filters, mask, prev, cur, gate]
    aliases = {}
    if so_far is not None:
        in_specs.append(pl.BlockSpec(memory_space=pl.ANY))
        operands.append(so_far)
        aliases = {5: 0}
    else:
        in_specs.append(pl.BlockSpec(memory_space=pl.ANY))
        operands.append(after)
    return pl.pallas_call(
        functools.partial(conv_kernel, groups),
        grid=(steps,),
        out_shape=jax.ShapeDtypeStruct(gate.shape, gate.dtype),
        in_specs=in_specs,
        out_specs=pl.BlockSpec((rows, lanes), lambda i: (0, first + i)),
        input_output_aliases=aliases,
        compiler_params=pltpu.CompilerParams(vmem_limit_bytes=VMEM_BYTES),
        cost_estimate=pl.CostEstimate(
            flops=DECLARED, bytes_accessed=DECLARED, transcendentals=0
        ),
    )(*operands)


def three_terms(x):
    high = x.astype(jnp.bfloat16).astype(jnp.float32)
    middle = (x - high).astype(jnp.bfloat16).astype(jnp.float32)
    return high, middle, x - high - middle


def attend_tiles(head, causal, use_far, q_ref, k_own, v_own, k_far, v_far, *refs):
    bias = refs[-1]
    out_ref = refs[-2]
    terms = out_ref.dtype == jnp.bfloat16
    stats = slice(out_ref.shape[1] - HEAD_DIM, out_ref.shape[1])
    place = pl.ds(pl.multiple_of(head * HEAD_DIM, HEAD_DIM), HEAD_DIM)
    own = k_own.shape[0]
    tile = 128
    count = q_ref.shape[0] // tile
    ones = jnp.ones((own, HEAD_DIM), jnp.bfloat16)
    wide_own = jnp.concatenate([v_own[...], ones], axis=1)
    wide_far = jnp.concatenate([v_far[...], ones], axis=1)
    lane = lax.broadcasted_iota(jnp.int32, (tile, HEAD_DIM), 1)

    def scores_of(i):
        here = slice(i * tile, (i + 1) * tile)
        seen = (i + 1) * tile if causal else own
        query = q_ref[here]
        dims = (((1,), (1,)), ((), ()))
        near = lax.dot_general(
            query, k_own[:seen], dims, preferred_element_type=jnp.float32
        )
        out = [near + bias[here, :seen]]
        if use_far:
            away = lax.dot_general(query, k_far[...], dims, preferred_element_type=jnp.float32)
            out.append(away + bias[here, own:])
        return out

    def finish(i, scores):
        here = slice(i * tile, (i + 1) * tile)
        top = jnp.max(scores[0], axis=1, keepdims=True)
        if use_far:
            top = jnp.maximum(top, jnp.max(scores[1], axis=1, keepdims=True))
        weights = [jnp.exp2((s - top) * SCALE2).astype(jnp.bfloat16) for s in scores]
        both = jnp.dot(
            weights[0], wide_own[: scores[0].shape[1]], preferred_element_type=jnp.float32
        )
        if use_far:
            both += jnp.dot(weights[1], wide_far, preferred_element_type=jnp.float32)
        total = both[:, HEAD_DIM:]
        out_ref[here, place] = (both[:, :HEAD_DIM] / total).astype(out_ref.dtype)
        lse = top * SCALE2 + jnp.log2(total)
        spread = out_ref[here, stats].astype(jnp.float32)
        if terms:
            for at, term in enumerate(three_terms(lse)):
                spread = jnp.where(lane == head + at * STEP, term, spread)
        else:
            spread = jnp.where(lane == head, lse, spread)
        out_ref[here, stats] = spread.astype(out_ref.dtype)

    ready = scores_of(0)
    for i in range(count):
        later = scores_of(i + 1) if i + 1 < count else None
        finish(i, ready)
        ready = later


def attend_kernel(causal, info_ref, *refs):
    how = info_ref[0]
    head = pl.program_id(0)
    refs = refs[:5] + refs[-2:]
    out_ref, bias = refs[-2:]
    rows, keys = bias.shape

    @pl.when((head == 0) & (how > 0))
    def _():
        stats = slice(out_ref.shape[1] - HEAD_DIM, out_ref.shape[1])
        out_ref[:, stats] = jnp.zeros((rows, HEAD_DIM), out_ref.dtype)
        at = info_ref[1] + lax.broadcasted_iota(jnp.int32, (rows, 1), 0)
        low = jnp.zeros_like(at)
        for doc in range(DOCS - 1):
            begin = info_ref[4 + doc]
            low = jnp.where(at >= begin, begin, low)
        lane = lax.broadcasted_iota(jnp.int32, (1, keys), 1)
        kpos = jnp.where(
            lane < keys // 2, info_ref[2] + lane, info_ref[3] + lane - keys // 2
        )
        allowed = (kpos >= low) & (kpos <= at)
        bias[...] = jnp.where(allowed, 0.0, NEG_FILL)

    if causal:

        @pl.when(how == 1)
        def _():
            attend_tiles(head, causal, False, *refs)

    @pl.when(how == 2)
    def _():
        attend_tiles(head, causal, True, *refs)


def attend(info, heads, causal, out_type, operands, after):
    rows = operands[0][0].shape[0]
    width = (heads + 1) * HEAD_DIM
    keys = operands[1][0].shape[0]

    def block(first, size):
        def at(h, info_ref):
            return (0, first + jnp.where(info_ref[0] > 0, h, 0))

        return pl.BlockSpec((size, HEAD_DIM), at)

    return pl.pallas_call(
        functools.partial(attend_kernel, causal),
        grid_spec=pltpu.PrefetchScalarGridSpec(
            num_scalar_prefetch=1,
            grid=(heads,),
            in_specs=[block(first, x.shape[0]) for x, first in operands]
            + [pl.BlockSpec(memory_space=pl.ANY)] * len(after),
            out_specs=pl.BlockSpec((rows, width), lambda h, info_ref: (0, 0)),
            scratch_shapes=[pltpu.VMEM((rows, 2 * keys), jnp.float32)],
        ),
        out_shape=jax.ShapeDtypeStruct((rows, width), out_type),
        compiler_params=pltpu.CompilerParams(vmem_limit_bytes=VMEM_BYTES),
        cost_estimate=pl.CostEstimate(
            flops=DECLARED, bytes_accessed=DECLARED, transcendentals=0
        ),
    )(info, *[x for x, _ in operands], *after)


def merge_kernel(each, chunks, has_ref, *refs):
    out_ref = refs[-1]
    has = has_ref[0]
    width = each * HEAD_DIM

    @pl.when(has == 0)
    def _():
        for c in range(chunks):
            out_ref[:, c * width : (c + 1) * width] = refs[2 * c][:, :width].astype(out_ref.dtype)

    @pl.when(has != 0)
    def _():
        for c in range(chunks):
            o1_ref, o2_ref = refs[2 * c : 2 * c + 2]
            mine = o1_ref[:, width:]
            sent = o2_ref[:, width:].astype(jnp.float32)
            second = (
                sent
                + pltpu.roll(sent, HEAD_DIM - STEP, 1)
                + pltpu.roll(sent, HEAD_DIM - 2 * STEP, 1)
            )
            top = jnp.maximum(mine, second)
            one, two = jnp.exp2(mine - top), jnp.exp2(second - top)
            share = two / (one + two)
            for h in range(each):
                cols = slice(h * HEAD_DIM, (h + 1) * HEAD_DIM)
                base = o1_ref[:, cols]
                mixed = base + (o2_ref[:, cols].astype(jnp.float32) - base) * share[:, h : h + 1]
                at = c * width + h * HEAD_DIM
                out_ref[:, at : at + HEAD_DIM] = mixed.astype(out_ref.dtype)


def merge(has, pairs, after):
    rows, wide = pairs[0][0].shape
    width = wide - HEAD_DIM
    vmem = pl.BlockSpec(memory_space=pltpu.VMEM)
    flat = [x for pair in pairs for x in pair]
    return pl.pallas_call(
        functools.partial(merge_kernel, width // HEAD_DIM, len(pairs)),
        out_shape=jax.ShapeDtypeStruct((rows, width * len(pairs)), jnp.bfloat16),
        in_specs=[pl.BlockSpec(memory_space=pltpu.SMEM)] + [vmem] * len(flat)
        + [pl.BlockSpec(memory_space=pl.ANY)],
        out_specs=vmem,
        compiler_params=pltpu.CompilerParams(vmem_limit_bytes=VMEM_BYTES),
        cost_estimate=pl.CostEstimate(
            flops=DECLARED, bytes_accessed=DECLARED, transcendentals=0
        ),
    )(has, *flat, after)


def on_device(mix_query, mix_key, mix_value, mr_filter, doc_ids, att_query, att_key, att_value):
    ctx = lax.axis_index("ctx")
    ctx_size = lax.axis_size("ctx")
    half = ctx_size // 2
    assert ctx_size == 4
    swap = [(i, i ^ 1) for i in range(ctx_size)]
    back = [(i + half, i) for i in range(half)]
    forth = [(i, i + half) for i in range(half)]

    rows, width = att_query.shape
    cut = width // 2
    low_pack = jnp.concatenate([att_key[:, :cut], att_value[:, :cut]], axis=1)
    high_pack = jnp.concatenate([att_key[:, cut:], att_value[:, cut:]], axis=1)
    on_first = ctx < half
    over = lax.ppermute(jnp.where(on_first, low_pack, att_query), "ctx", forth + back)
    low_swap = lax.ppermute(low_pack, "ctx", swap)
    high_swap = lax.ppermute(high_pack, "ctx", swap)

    tok_rows, channels = mix_query.shape
    chunk = channels // MIX_CHUNKS
    peers = ctx_size * lax.axis_size("head")
    onward = [(i, i + 1) for i in range(peers - 1)]
    products, rims = [], []
    for c in range(MIX_CHUNKS):
        cols = slice(c * chunk, (c + 1) * chunk)
        product = (
            mix_key[:, cols].astype(jnp.float32) * mix_value[:, cols].astype(jnp.float32)
        ).astype(jnp.bfloat16)
        products.append(product)
        rims.append(lax.ppermute(product, ("ctx", "head"), onward))
    begins = [
        jnp.sum((doc_ids < doc).astype(jnp.int32), dtype=jnp.int32) for doc in range(1, DOCS)
    ]

    def info(how, query_block, own_block, other_block):
        blocks = [x * rows for x in (query_block, own_block, other_block)]
        return jnp.stack([jnp.asarray(x, jnp.int32) for x in [how] + blocks + begins])

    each = width // 2 // HEAD_DIM
    local_info = info(jnp.where(ctx % 2 == 1, 2, 1), ctx, ctx, ctx ^ 1)
    high_info = info(jnp.where(on_first, 2, 0), ctx + half, ctx, ctx ^ 1)
    low_info = info(jnp.where(on_first, 0, 2), ctx, ctx - half, (ctx - half) ^ 1)

    local_low = attend(
        local_info,
        each,
        True,
        jnp.float32,
        [(att_query, 0), (att_key, 0), (att_value, 0), (low_swap, 0), (low_swap, each)],
        (),
    )
    local_high = attend(
        local_info,
        each,
        True,
        jnp.float32,
        [(att_query, each), (att_key, each), (att_value, each), (high_swap, 0), (high_swap, each)],
        (local_low,),
    )
    over, local_high = lax.optimization_barrier((over, local_high))
    cross = lax.ppermute(over, "ctx", swap[half:])
    far_high = attend(
        high_info,
        each,
        False,
        jnp.bfloat16,
        [(over, each), (att_key, each), (att_value, each), (high_swap, 0), (high_swap, each)],
        (local_high,),
    )
    high_forth = lax.ppermute(far_high, "ctx", forth)
    far_low = attend(
        low_info,
        each,
        False,
        jnp.bfloat16,
        [(att_query, 0), (over, 0), (over, each), (cross, 0), (cross, each)],
        (far_high, rims[0]),
    )
    has = (ctx >= half).astype(jnp.int32)[None]

    taps = mr_filter.shape[1]
    place = (ctx * lax.axis_size("head") + lax.axis_index("head")) * tok_rows
    padded_ids = jnp.concatenate([jnp.full((taps,), -1, jnp.int32), doc_ids])
    near_ids = lax.dynamic_slice_in_dim(padded_ids, place, tok_rows + taps)
    lag = jnp.arange(tok_rows)[None, :] + taps - jnp.arange(tok_rows + taps)[:, None]
    mask = (
        (lag >= 0) & (lag < taps) & (near_ids[:, None] == near_ids[None, taps:])
    ).astype(jnp.bfloat16)
    mixed = None
    for c in range(MIX_CHUNKS):
        mixed = convolve(c, mr_filter, mask, rims[c], products[c], mix_query, mixed, far_low)
    attended = merge(has, [(local_low, far_low), (local_high, high_forth)], mixed)
    return (mixed, attended)


def solution(mesh):
    placed = (
        P(("dp", "ctx", "head"), None),
        P(("dp", "ctx", "head"), None),
        P(("dp", "ctx", "head"), None),
        P(),
        P("dp"),
        P(("dp", "ctx"), "head"),
        P(("dp", "ctx"), "head"),
        P(("dp", "ctx"), "head"),
    )
    return jax.shard_map(
        on_device,
        mesh=mesh,
        in_specs=placed,
        out_specs=(P(("dp", "ctx", "head"), None), P(("dp", "ctx"), "head")),
        check_vma=False,
    )
```
